32 devices in a mesh: row: 8 (over y, x, core), col: 4 (over z).
Axes of the slice: x: 2, y: 2, z: 4, core: 2. Of those that a mesh axis runs over, the one named last changes fastest.
Arguments:
- x_src: bfloat16 [50, 4096], P(None, ('row', 'col')), may hold values from -2.5 to 2.5
- y_tgt: bfloat16 [50, 8192], P(None, ('row', 'col')), may hold values from -2.5 to 2.5
- a_src: bfloat16 [4096], P(('row', 'col')), may hold values from 0.099609375 to 10
- b_tgt: bfloat16 [8192], P(('row', 'col')), may hold values from 0.099609375 to 10
Outputs:
- proj_src: float32 [50, 4096], P(None, ('row', 'col'))
- proj_tgt: float32 [50, 8192], P(None, ('row', 'col'))
The draws below stay inside these ranges and needn't reach their ends.
All inputs are finite; a program needn't handle non-finite values.
Results may differ from the reference program's by a relative error of at most 0.0045.
Values may be sent and summed in bfloat16 or wider, within the bound.
No kernel may reach another device: no remote copies, remote signals or barrier semaphores. Data moves between devices by JAX's collectives and lax.ppermute only.
A program may use at most 64 MiB of HBM per device.

```python
import math
import jax
import jax.numpy as jnp
from jax import lax

D = 50
SR = 512
ITERS = 2
NS = 4096
NT = 8192


def level_of(rng, shape, pieces, smallest, high):
    gain = 1.0
    for dim, parts in pieces:
        heights = jax.random.uniform(jax.random.fold_in(jax.random.fold_in(rng, 6), dim), (parts,), jnp.float32, smallest / len(pieces), high / len(pieces))
        gain = gain * jnp.repeat(jnp.exp(heights), shape[dim] // parts).reshape((-1,) + (1,) * (len(shape) - 1 - dim))
    return gain


def centred(key, shape, spread, reach, shards=(), held_as=jnp.bfloat16):
    values = spread * jax.random.normal(key, shape, jnp.float32)
    if shards:
        values = values * level_of(key, shape, shards, -0.22, 0.18)
    return jnp.clip(values, -reach, reach).astype(held_as)


def setup_inputs(seed: int = 0) -> dict:
    splits = jax.random.split(jax.random.key(seed), 5)
    return {
        "x_src": centred(splits[0], (D, NS), 1.0, 2.5, ((1, 32),)),
        "y_tgt": centred(splits[1], (D, NT), 1.0, 2.5, ((1, 32),)),
        "a_src": jnp.clip(jnp.exp(math.log(10.0) - 4.609084 * jax.random.uniform(splits[2], (NS,), jnp.float32) ** level_of(splits[2], (NS,), ((0, 32),), -0.2, 0.2)), 0.099609375, 10.0).astype(jnp.bfloat16),
        "b_tgt": jnp.clip(jnp.exp(math.log(10.0) - 4.609084 * jax.random.uniform(splits[3], (NT,), jnp.float32) ** level_of(splits[3], (NT,), ((0, 32),), -0.2, 0.2)), 0.099609375, 10.0).astype(jnp.bfloat16),
    }


EPSILON_KERNEL = 0.05


def kernel_rows(xb, xnb, coords, ynorm):
    cross = lax.dot_general(xb, coords, (((0,), (0,)), ((), ())), preferred_element_type=jnp.float32)
    return jnp.exp(-(xnb[:, None] + ynorm[None, :] - 2.0 * cross) / (2.0 * D * EPSILON_KERNEL))


def reference(x_src, y_tgt, a_src, b_tgt):
    hi = lax.Precision.HIGHEST
    xnorm = jnp.sum(jnp.square(x_src.astype(jnp.float32)), axis=0)
    ynorm = jnp.sum(jnp.square(y_tgt.astype(jnp.float32)), axis=0)
    blocks = NS // SR
    xs = x_src.reshape(D, blocks, SR).transpose(1, 0, 2)
    xns = xnorm.reshape(blocks, SR)
    a_full = a_src.astype(jnp.float32)
    b_full = b_tgt.astype(jnp.float32)

    def row_sums(later_dual_vector):
        def one(t):
            return jnp.dot(kernel_rows(t[0], t[1], y_tgt, ynorm), later_dual_vector, precision=hi)
        return lax.map(one, (xs, xns)).reshape(NS)

    def col_sums(earlier_dual_vector):
        us = earlier_dual_vector.reshape(blocks, SR)

        def step(carry, t):
            xb, xnb, ub = t
            kern = kernel_rows(xb, xnb, y_tgt, ynorm)
            total = carry[0] + jnp.dot(ub, kern, precision=hi)
            cell_weights = (ub[:, None] * kern).astype(jnp.bfloat16)
            numer = carry[1] + jnp.dot(xb, cell_weights, preferred_element_type=jnp.float32)
            return (total, numer), None

        init = (jnp.zeros((NT,), jnp.float32), jnp.zeros((D, NT), jnp.float32))
        return lax.scan(step, init, (xs, xns, us))[0]

    later_dual_vector = jnp.ones((NT,), jnp.float32)
    for step in range(ITERS):
        earlier_dual_vector = a_full / row_sums(later_dual_vector)
        total, numer = col_sums(earlier_dual_vector)
        later_dual_vector = b_full / total
    proj_tgt = numer / total[None, :]

    def final(t):
        kern = kernel_rows(t[0], t[1], y_tgt, ynorm)
        den = jnp.dot(kern, later_dual_vector, precision=hi)
        cell_weights = (kern * later_dual_vector[None, :]).astype(jnp.bfloat16)
        num = lax.dot_general(y_tgt, cell_weights, (((1,), (1,)), ((), ())), preferred_element_type=jnp.float32)
        return den, num

    dens, nums = lax.map(final, (xs, xns))
    den_all = dens.reshape(NS)
    num_all = nums.transpose(1, 0, 2).reshape(D, NS)
    proj_src = num_all / den_all[None, :]
    return proj_src, proj_tgt
```

```python
import jax
import jax.numpy as jnp
import numpy as np
from jax import lax
from jax.experimental import pallas as pl
from jax.experimental.pallas import tpu as pltpu
from jax.sharding import PartitionSpec as P

D = 50
EPSILON_KERNEL = 0.05
SCALE = float(2.0 / (2.0 * D * EPSILON_KERNEL) / np.log(2.0))
EXT = 56
NORM_X, NORM_Y, B_ROW, A_ROW = D, D + 2, D + 4, D + 5

f32 = jnp.float32
bf16 = jnp.bfloat16
VM = pl.BlockSpec(memory_space=pltpu.VMEM)
SM = pl.BlockSpec(memory_space=pltpu.SMEM)


def params():
    return pltpu.CompilerParams(vmem_limit_bytes=40 * 2**20)


def ext_kernel(x_ref, y_ref, a_ref, b_ref, o_ref, sx, sy):
    nx = x_ref.shape[1]
    for src, w, s, norm, one, w_row in (
        (x_ref, a_ref, sx, NORM_X, NORM_Y, A_ROW),
        (y_ref, b_ref, sy, NORM_Y, NORM_X, B_ROW),
    ):
        c = src[...].astype(f32)
        n = -0.5 * jnp.sum(c * c, axis=0, keepdims=True)
        hi = n.astype(bf16).astype(f32)
        s[...] = jnp.zeros_like(s)
        s[0:D, :] = c
        s[norm : norm + 1, :] = hi
        s[norm + 1 : norm + 2, :] = n - hi
        s[one : one + 2, :] = jnp.ones((2, s.shape[1]), f32)
        s[w_row : w_row + 1, :] = w[...].astype(f32)
    o_ref[:, 0:nx] = sx[...].astype(bf16)
    o_ref[:, nx:] = sy[...].astype(bf16)


def kernel_block(xt, y):
    s = lax.dot_general(xt, y, (((1,), (0,)), ((), ())), preferred_element_type=f32)
    return jnp.exp2(s * SCALE)


def add_lanes(acc, e):
    for t in range(e.shape[1] // 128):
        acc = acc + e[:, t * 128 : (t + 1) * 128]
    return acc


def make_blocks(xt, ys, ks, acc):
    for i, y in enumerate(ys):
        e = kernel_block(xt, y[...])
        if ks:
            ks[i][...] = e
        acc = add_lanes(acc, e)
    return acc


def block(i, ks, xt_ref, ys, rows=slice(None), cols=slice(None)):
    if ks:
        return ks[i][rows, cols]
    return kernel_block(xt_ref[rows, :], ys[i][:, cols])


def first_kernel(n, xe_ref, *refs):
    ys, (xt_ref, acc_ref), ks = refs[:n], refs[n : n + 2], refs[n + 2 :]
    xt = jnp.transpose(xe_ref[...].astype(f32)).astype(bf16)
    xt_ref[...] = xt
    acc_ref[...] = make_blocks(xt, ys, ks, jnp.zeros(acc_ref.shape, f32))


def next_kernel(n, xt_ref, acc0_ref, *refs):
    ys, acc_ref, ks = refs[:n], refs[n], refs[n + 1 :]
    acc_ref[...] = make_blocks(xt_ref[...], ys, ks, acc0_ref[...])


def col_sums(rows, ks, xt_ref, ys, u, tot, r):
    for i in range(rows):
        e = block(i, ks, xt_ref, ys)
        tot[pl.ds(r ^ i, 1), :] = jnp.sum(e * u, axis=0, keepdims=True)


def last_kernel(n, rows, kept, r_ref, xt_ref, acc0_ref, *refs):
    n_y = n if kept else rows
    n_k = rows - n if kept else 0
    ys, old = refs[:n_y], refs[n_y : n_y + n_k]
    o_ref, new, tot = refs[n_y + n_k], refs[n_y + n_k + 1 : -1], refs[-1]
    late = range(3, rows, 2)
    acc = make_blocks(xt_ref[...], ys[-n:], new, acc0_ref[...])
    ks = [None] * rows if kept else ()
    if kept:
        for i, k in zip([0, 1, *range(2, rows, 2), *late], [*old, *new]):
            ks[i] = k
    else:
        ys = order(ys, rows)
    u = xt_ref[:, A_ROW : A_ROW + 1].astype(f32) / jnp.sum(acc, axis=1, keepdims=True)
    col_sums(rows, ks, xt_ref, ys, u, tot, r_ref[0])
    t = tot[...].astype(bf16)
    for e in range(rows):
        o_ref[e] = t


def order(blocks, rows):
    made = [0, 1, *range(2, rows, 2), *range(3, rows, 2)]
    return [blocks[made.index(i)] for i in range(rows)]


def second_kernel(rows, own, width, r_ref, got_ref, xt_ref, xe_ref, *refs):
    ys, ks = refs[:rows], refs[rows:-2]
    o_ref, tot = refs[-2:]
    r = r_ref[0]
    tot[...] = jnp.sum(got_ref[...].astype(f32), axis=0)
    acc = jnp.zeros((xt_ref.shape[0], 128), f32)
    for i in range(rows):
        v = ys[i][B_ROW : B_ROW + 1, :].astype(f32) / tot[pl.ds(r ^ i, 1), :]
        acc = add_lanes(acc, block(i, ks, xt_ref, ys) * v)
    u = xt_ref[:, A_ROW : A_ROW + 1].astype(f32) / jnp.sum(acc, axis=1, keepdims=True)
    col_sums(rows, ks, xt_ref, ys, u, tot, r)
    t = jnp.concatenate(
        [tot[:, g : g + width] for g in range(0, tot.shape[1], width)], axis=0
    ).astype(bf16)
    x = xe_ref[...]
    for i in range(rows):
        z = (block(i, ks, xt_ref, ys, cols=slice(0, own)) * u).astype(bf16)
        num = jnp.dot(x, z, preferred_element_type=f32)
        o_ref[r ^ i, 0 : t.shape[0], :] = t
        o_ref[r ^ i, t.shape[0] :, 0:own] = num.astype(bf16)


def final_kernel(rows, own_x, own, width, r_ref, got_ref, xt_ref, *refs):
    ys, ks = refs[:rows], refs[rows:-4]
    src_ref, tgt_ref, tot, num_s = refs[-4:]
    r = r_ref[0]
    s = jnp.sum(got_ref[...].astype(f32), axis=0)
    for g in range(tot.shape[1] // width):
        tot[:, g * width : (g + 1) * width] = s[g * rows : (g + 1) * rows, :]
    num_s[...] = s[rows * tot.shape[1] // width :, 0:own]
    tgt_ref[...] = num_s[0:D, :] / tot[pl.ds(r, 1), :][:, 0:own]
    num = jnp.zeros((EXT, own_x), f32)
    for i in range(rows):
        v = ys[i][B_ROW : B_ROW + 1, :].astype(f32) / tot[pl.ds(r ^ i, 1), :]
        w = (block(i, ks, xt_ref, ys, rows=slice(0, own_x)) * v).astype(bf16)
        num = num + lax.dot_general(
            ys[i][...], w, (((1,), (1,)), ((), ())), preferred_element_type=f32
        )
    src_ref[...] = num[0:D, :] / num[NORM_X : NORM_X + 1, :]


def xor_perm(n, m):
    return [(i, i ^ m) for i in range(n)]


def solution(mesh):
    rows, cols = mesh.shape["row"], mesh.shape["col"]

    def per_device(x_src, y_tgt, a_src, b_tgt):
        nx, ny = x_src.shape[1], y_tgt.shape[1]
        S, T = nx * cols, ny * cols
        kept = S * T * rows * 4 <= 24 * 2**20

        def held(shape, dtype):
            if kept:
                return pltpu.VMEM(shape, dtype)
            return jax.ShapeDtypeStruct(shape, dtype)

        def call(kernel, outs, n_in, scratch=(), smem=0, cost=None):
            return pl.pallas_call(
                kernel,
                out_shape=outs,
                in_specs=[SM] * smem + [VM] * n_in,
                out_specs=jax.tree.map(lambda _: VM, outs),
                scratch_shapes=scratch,
                compiler_params=params(),
                cost_estimate=cost,
            )

        r = lax.axis_index("row").astype(jnp.int32).reshape(1)
        p = call(
            ext_kernel,
            jax.ShapeDtypeStruct((EXT, nx + ny), bf16),
            4,
            [pltpu.VMEM((EXT, nx), f32), pltpu.VMEM((EXT, ny), f32)],
        )(x_src, y_tgt, a_src.reshape(1, nx), b_tgt.reshape(1, ny))
        ps = [p] + [
            lax.ppermute(p, "col", xor_perm(cols, m)) for m in range(1, cols)
        ]
        y = [None] * rows
        y[0] = jnp.concatenate([q[:, nx:] for q in ps], axis=1)
        for m in range(2, rows, 2):
            y[m] = lax.ppermute(y[0], "row", xor_perm(rows, m))
        for m in range(0, rows, 2):
            y[m + 1] = lax.ppermute(y[m], "row", xor_perm(rows, 1))
        xe = jnp.concatenate([q[:, :nx] for q in ps], axis=1)

        def cost(n):
            return pl.CostEstimate(
                flops=2 * EXT * S * T * n,
                bytes_accessed=S * T * n,
                transcendentals=S * T * n,
            )

        acc_t = held((S, 128), f32)
        k_t = held((S, T), f32)
        k_n = 1 if kept else 0
        n = rows // 2 - 1
        evens, odds = range(2, rows, 2), range(3, rows, 2)
        xt, acc, *made = call(
            lambda *refs: first_kernel(2, *refs),
            (held((S, EXT), bf16), acc_t) + (k_t,) * (2 * k_n),
            3,
            cost=cost(2),
        )(xe, y[0], y[1])
        acc, *new = call(
            lambda *refs: next_kernel(n, *refs),
            (acc_t,) + (k_t,) * (n * k_n),
            2 + n,
            cost=cost(n),
        )(xt, acc, *[y[m] for m in evens])
        made += new
        late = [y[m] for m in odds]
        if not kept:
            late = [y[0], y[1]] + [y[m] for m in evens] + late
        send, *new = call(
            lambda *refs: last_kernel(n, rows, kept, *refs),
            (jax.ShapeDtypeStruct((rows, rows, T), bf16),) + (k_t,) * (n * k_n),
            2 + len(late) + len(made),
            [pltpu.VMEM((rows, T), f32)],
            smem=1,
            cost=cost(n),
        )(r, xt, acc, *late, *made)
        ks = order(made + new, rows) if kept else []
        got = lax.all_to_all(send, "row", 0, 0)
        width = max(ny, 128)
        n_tot = rows * T // width
        send = call(
            lambda *refs: second_kernel(rows, ny, width, *refs),
            jax.ShapeDtypeStruct((rows, n_tot + EXT, width), bf16),
            3 + rows + len(ks),
            [pltpu.VMEM((rows, T), f32)],
            smem=1,
        )(r, got, xt, xe, *y, *ks)
        got = lax.all_to_all(send, "row", 0, 0)
        return tuple(
            call(
                lambda *refs: final_kernel(rows, nx, ny, width, *refs),
                (
                    jax.ShapeDtypeStruct((D, nx), f32),
                    jax.ShapeDtypeStruct((D, ny), f32),
                ),
                2 + rows + len(ks),
                [pltpu.VMEM((rows, T), f32), pltpu.VMEM((EXT, ny), f32)],
                smem=1,
            )(r, got, xt, *y, *ks)
        )

    spec = P(None, ("row", "col"))
    vec = P(("row", "col"))
    return jax.shard_map(
        per_device,
        mesh=mesh,
        in_specs=(spec, spec, vec, vec),
        out_specs=(spec, spec),
        check_vma=False,
    )
```

```python
import jax
import jax.numpy as jnp
import numpy as np
from jax import lax
from jax.experimental import pallas as pl
from jax.experimental.pallas import tpu as pltpu
from jax.sharding import PartitionSpec as P

D = 50
EPSILON_KERNEL = 0.05
SCALE = float(2.0 / (2.0 * D * EPSILON_KERNEL) / np.log(2.0))
EXT = 56
NORM_X, NORM_Y, B_ROW, A_ROW = D, D + 2, D + 4, D + 5
LANES, SUB = 128, 8
VMEM_BYTES = 16 * 2**20

f32 = jnp.float32
bf16 = jnp.bfloat16
VM = pl.BlockSpec(memory_space=pltpu.VMEM)
ANY = pl.BlockSpec(memory_space=pl.ANY)


def ext_kernel(x_hbm, y_hbm, a_hbm, b_hbm, o_ref, xv, yv, av, bv, sx, sy, sems):
    copies = [
        pltpu.make_async_copy(src, dst, sems.at[i])
        for i, (src, dst) in enumerate(
            ((x_hbm, xv), (y_hbm, yv), (a_hbm, av), (b_hbm, bv))
        )
    ]
    for c in copies:
        c.start()
    for c in copies:
        c.wait()
    ny = yv.shape[1]
    for src, w, s, norm, one, w_row in (
        (xv, av, sx, NORM_X, NORM_Y, A_ROW),
        (yv, bv, sy, NORM_Y, NORM_X, B_ROW),
    ):
        c = src[...].astype(f32)
        n = -0.5 * jnp.sum(c * c, axis=0, keepdims=True)
        hi = n.astype(bf16).astype(f32)
        s[...] = jnp.zeros_like(s)
        s[0:D, :] = c
        s[norm : norm + 1, :] = hi
        s[norm + 1 : norm + 2, :] = n - hi
        s[one : one + 2, :] = jnp.ones((2, s.shape[1]), f32)
        s[w_row : w_row + 1, :] = w[...].astype(f32).reshape(1, -1)
    o_ref[:, 0:ny] = sy[...].astype(bf16)
    o_ref[:, ny:] = sx[...].astype(bf16)


def kernel_block(xt, y):
    s = lax.dot_general(xt, y, (((1,), (0,)), ((), ())), preferred_element_type=f32)
    return jnp.exp2(s * SCALE)


def add_lanes(acc, e):
    for t in range(e.shape[1] // LANES):
        acc = acc + e[:, t * LANES : (t + 1) * LANES]
    return acc


def spread(v, width):
    return jnp.concatenate([v] * (width // LANES), axis=1)


def groups(rows, body, init=0):
    n = rows // SUB

    def step(i, carry):
        return body(pl.ds(pl.multiple_of(i * SUB, SUB), SUB), carry)

    return lax.fori_loop(0, n, step, init, unroll=min(8, n))


def row_pass(k, v, acc):
    vb = jnp.broadcast_to(v, (SUB, v.shape[1]))

    def body(rs, carry):
        acc[rs, :] = add_lanes(acc[rs, :], k[rs, :] * vb)
        return carry

    groups(k.shape[0], body)


def col_pass(k, u, init):
    def body(rs, carry):
        return carry + k[rs, :] * spread(u[rs, :], carry.shape[1])

    return groups(k.shape[0], body, init)


def scaling(weights, acc, u):
    u[...] = weights[...] / jnp.broadcast_to(
        jnp.sum(acc[...], axis=1, keepdims=True), u.shape
    )


class Refs:
    def __init__(self, refs):
        self.refs = list(refs)

    def take(self, *counts):
        out = []
        for n in counts:
            out.append(self.refs[:n] if isinstance(n, int) else self.refs[: n[0]][0])
            del self.refs[: n if isinstance(n, int) else n[0]]
        return out


ONE = (1,)


def xor_perm(n, m):
    return [(i, i ^ m) for i in range(n)]


def solution(mesh):
    rows, cols = mesh.shape["row"], mesh.shape["col"]

    def per_device(x_src, y_tgt, a_src, b_tgt):
        nx, ny = x_src.shape[1], y_tgt.shape[1]
        X, T = nx * cols, ny * cols
        def slab(split):
            return rows // split * X * T * rows * 4

        split = 4 if slab(4) <= 36 * 2**20 else rows
        kept = slab(split) <= 36 * 2**20
        parts = rows // split
        bits = split.bit_length() - 1
        width = max(ny, LANES)
        per_row = T // width

        def held(shape, dtype):
            return pltpu.VMEM(shape, dtype) if kept else jax.ShapeDtypeStruct(shape, dtype)

        def call(kernel, outs, args, scratch=(), cost=None, spec=VM):
            return pl.pallas_call(
                kernel,
                out_shape=outs,
                in_specs=[spec] * len(args),
                out_specs=jax.tree.map(lambda _: VM, outs),
                scratch_shapes=scratch,
                compiler_params=pltpu.CompilerParams(vmem_limit_bytes=VMEM_BYTES),
                cost_estimate=cost,
            )(*args)

        def cost(n):
            return pl.CostEstimate(
                flops=2 * EXT * X * T * n,
                bytes_accessed=X * T * n,
                transcendentals=X * T * n,
            )

        block_t = held((X, T), f32)
        lanes_t = held((X, LANES), f32)
        block_s = pltpu.VMEM((X, T), f32)
        lanes_s = pltpu.VMEM((X, LANES), f32)
        tot_t = jax.ShapeDtypeStruct((rows, T), f32)

        def blocks(ks, xts, ys, spare=None):
            def get(q, i):
                if kept:
                    return ks[q * rows + i]
                spare[...] = kernel_block(xts[q][...], ys[i][:, 0:T])
                return spare

            return get

        spare = [] if kept else [block_s]

        own = call(
            ext_kernel,
            jax.ShapeDtypeStruct((EXT, ny + nx), bf16),
            [
                pltpu.with_memory_space_constraint(t, pltpu.HBM)
                for t in (x_src, y_tgt, a_src, b_tgt)
            ],
            [
                pltpu.VMEM((D, nx), bf16),
                pltpu.VMEM((D, ny), bf16),
                pltpu.VMEM((nx,), bf16),
                pltpu.VMEM((ny,), bf16),
                pltpu.VMEM((EXT, nx), f32),
                pltpu.VMEM((EXT, ny), f32),
                pltpu.SemaphoreType.DMA((4,)),
            ],
            spec=ANY,
        )
        line = [own] + [
            lax.ppermute(own, "col", xor_perm(cols, m)) for m in range(1, cols)
        ]
        both = jnp.concatenate(
            [p[:, 0:ny] for p in line] + [p[:, ny:] for p in line], axis=1
        )
        y0 = both[:, 0:T]
        y, xe = [None] * rows, [None] * parts
        y[0], xe[0] = y0, both[:, T:]
        for m in range(2, rows, 2):
            if m % split == 0:
                w = lax.ppermute(both, "row", xor_perm(rows, m))
                y[m], xe[m // split] = w[:, 0:T], w[:, T:]
            else:
                y[m] = lax.ppermute(y0, "row", xor_perm(rows, m))
        for m in range(0, rows, 2):
            y[m + 1] = lax.ppermute(y[m], "row", xor_perm(rows, 1))

        k_all = [None] * (parts * rows)
        xts, abs_, accs = [None] * parts, [None] * parts, [None] * parts

        def make(new, todo, ys, extra):
            old = sorted({q for q, _ in todo} - set(new))

            def kernel(*refs):
                r = Refs(refs)
                xe_r, xt_r, acc_r, y_r = r.take(len(new), len(old), len(old), len(ys))
                xt_o, ab_o, acc_o, k_o = r.take(
                    len(new), len(new), len(new) + len(old), len(todo) if kept else 0
                )
                xt = dict(zip(old, xt_r))
                accs_in = {q: a[...] for q, a in zip(old, acc_r)}
                for q, e, t, ab in zip(new, xe_r, xt_o, ab_o):
                    t[...] = jnp.transpose(e[...].astype(f32)).astype(bf16)
                    xt[q] = t
                    ab[...] = jnp.broadcast_to(
                        t[:, A_ROW : A_ROW + 1].astype(f32), ab.shape
                    )
                    accs_in[q] = jnp.zeros((X, LANES), f32)
                y_of = dict(zip(ys, y_r))
                for n, (q, i) in enumerate(todo):
                    e = kernel_block(xt[q][...], y_of[i][...])
                    if kept:
                        k_o[n][...] = e
                    accs_in[q] = add_lanes(accs_in[q], e)
                for q, o in zip(new + old, acc_o):
                    o[...] = accs_in[q]

            outs = (
                [held((X, EXT), bf16)] * len(new)
                + [lanes_t] * (2 * len(new) + len(old))
                + ([block_t] * len(todo) if kept else [])
            )
            args = (
                [xe[q] for q in new]
                + [xts[q] for q in old]
                + [accs[q] for q in old]
                + [y[i] for i in ys]
            )
            got = Refs(call(kernel, outs, args, cost=cost(len(todo))))
            new_xt, new_ab, new_acc, new_k = got.take(
                len(new), len(new), len(new) + len(old), len(todo) if kept else 0
            )
            for q, t, ab in zip(new, new_xt, new_ab):
                xts[q], abs_[q] = t, ab
            for q, acc in zip(new + old, new_acc):
                accs[q] = acc
            for (q, i), k in zip(todo, new_k):
                k_all[q * rows + i] = k

        evens, odds = list(range(2, rows, 2)), list(range(3, rows, 2))
        rest = list(range(1, parts))
        make([0], [(0, 0), (0, 1)], [0, 1], None)
        make(
            rest,
            [(q, i) for q in range(parts) for i in ([] if q == 0 else [0, 1]) + evens],
            ([0, 1] if rest else []) + evens,
            None,
        )
        make([], [(q, i) for q in range(parts) for i in odds], odds, None)
        ks = k_all if kept else []
        matrix = [] if kept else [*xts, *y]

        def matrix_refs(r):
            if kept:
                return r.take(parts * rows)[0], (), ()
            xt, ys = r.take(parts, rows)
            return (), xt, ys

        def col_sums(get, us, tot):
            for i in range(rows):
                s = jnp.zeros((SUB, T), f32)
                for q in range(parts):
                    s = col_pass(get(q, i), us[q], s)
                tot[i : i + 1, :] = jnp.sum(s, axis=0, keepdims=True)

        def first_sums(*refs):
            r = Refs(refs)
            acc, ab = r.take(parts, parts)
            k, xt, ys = matrix_refs(r)
            tot, us = r.take(ONE, parts)
            get = blocks(k, xt, ys, *r.refs)
            for q in range(parts):
                scaling(ab[q], acc[q], us[q])
            col_sums(get, us, tot)

        tot = call(
            first_sums,
            tot_t,
            [*accs, *abs_, *ks, *matrix],
            [lanes_s] * parts + spare,
        )

        def add_swapped(t, g, m):
            return jnp.concatenate(
                [t[i : i + 1] + g[i ^ m : (i ^ m) + 1] for i in range(rows)], axis=0
            )

        def add_kernel(m):
            def kernel(t, g, o):
                o[...] = add_swapped(t[...], g[...], m)

            return kernel

        for b in range(bits):
            got = lax.ppermute(tot, "row", xor_perm(rows, 1 << b))
            if b < bits - 1:
                tot = call(add_kernel(1 << b), tot_t, [tot, got])

        n_tot = rows * per_row

        def pack_tot(t):
            return jnp.concatenate(
                [t[:, g * width : (g + 1) * width] for g in range(per_row)], axis=0
            ).astype(bf16)

        def unpack_tot(s):
            s = s.astype(f32)
            return jnp.concatenate(
                [s[g * rows : (g + 1) * rows, :] for g in range(per_row)], axis=1
            )

        def second(*refs):
            r = Refs(refs)
            t, g, ab, xes, bs = r.take(ONE, ONE, parts, parts, rows if kept else 0)
            k, xt, ys = matrix_refs(r)
            bs = bs or ys
            tot_o, keep_o, send_o, acc, us = r.take(ONE, ONE, ONE, ONE, parts)
            get = blocks(k, xt, ys, *r.refs)
            total = add_swapped(t[...], g[...], split // 2)
            v = [
                bs[i][B_ROW : B_ROW + 1, 0:T].astype(f32) / total[i : i + 1, :]
                for i in range(rows)
            ]
            for q in range(parts):
                acc[...] = jnp.zeros_like(acc)
                for i in range(rows):
                    row_pass(get(q, i), v[i], acc)
                scaling(ab[q], acc, us[q])
            col_sums(get, us, tot_o)
            send_o[0:n_tot, :] = pack_tot(tot_o[...])
            for i in range(split):
                num = jnp.zeros((EXT, ny), f32)
                for q in range(parts):
                    z = get(q, i)[:, 0:ny] * spread_to(us[q][...], ny)
                    num = num + jnp.dot(
                        xes[q][...], z.astype(bf16), preferred_element_type=f32
                    )
                if i % 2 == 0:
                    keep_o[i // 2, :, 0:ny] = num
                else:
                    at = n_tot + i // 2 * EXT
                    send_o[at : at + EXT, 0:ny] = num.astype(bf16)

        def spread_to(u, n):
            return u[:, 0:n] if n <= LANES else spread(u, n)

        half = split // 2
        tot, keep, send = call(
            second,
            (
                tot_t,
                jax.ShapeDtypeStruct((half, EXT, width), f32),
                jax.ShapeDtypeStruct((n_tot + half * EXT, width), bf16),
            ),
            [tot, got, *abs_, *xe, *(y if kept else []), *ks, *matrix],
            [lanes_s] * (1 + parts) + spare,
        )

        def halve(m):
            def kernel(t, kp, g, tot_o, keep_o, send_o):
                tot_o[...] = add_swapped(t[...], unpack_tot(g[0:n_tot, :]), m)
                send_o[0:n_tot, :] = pack_tot(tot_o[...])
                for j in range(kp.shape[0]):
                    s = kp[j] + g[n_tot + j * EXT : n_tot + (j + 1) * EXT, :].astype(f32)
                    if j % 2 == 0:
                        keep_o[j // 2] = s
                    else:
                        at = n_tot + j // 2 * EXT
                        send_o[at : at + EXT, :] = s.astype(bf16)

            return kernel

        for b in range(bits):
            got = lax.ppermute(send, "row", xor_perm(rows, 1 << b))
            if b < bits - 1:
                half //= 2
                tot, keep, send = call(
                    halve(1 << b),
                    (
                        tot_t,
                        jax.ShapeDtypeStruct((half, EXT, width), f32),
                        jax.ShapeDtypeStruct((n_tot + half * EXT, width), bf16),
                    ),
                    [tot, keep, got],
                )

        def final(*refs):
            r = Refs(refs)
            t, kp, g, xt, ys = r.take(ONE, ONE, ONE, ONE, rows)
            k = r.take(rows if kept else 0)[0]
            src_o, tgt_o = r.take(ONE, ONE)
            total = add_swapped(t[...], unpack_tot(g[0:n_tot, :]), split // 2)
            num = kp[0] + g[n_tot:, :].astype(f32)
            tgt_o[...] = num[0:D, 0:ny] / total[0:1, 0:ny]
            res = jnp.zeros((nx, EXT), f32)
            for i in range(rows):
                yi = ys[i][:, 0:T]
                v = yi[B_ROW : B_ROW + 1, :].astype(f32) / total[i : i + 1, :]
                e = k[i][0:nx, :] if kept else kernel_block(xt[0:nx, :], yi)
                res = res + lax.dot_general(
                    (e * v).astype(bf16),
                    yi,
                    (((1,), (1,)), ((), ())),
                    preferred_element_type=f32,
                )
            res = jnp.transpose(res)
            src_o[...] = res[0:D, :] / res[NORM_X : NORM_X + 1, :]

        return tuple(
            call(
                final,
                (
                    jax.ShapeDtypeStruct((D, nx), f32),
                    jax.ShapeDtypeStruct((D, ny), f32),
                ),
                [tot, keep, got, xts[0], *y, *(ks[0:rows] if kept else [])],
            )
        )

    spec = P(None, ("row", "col"))
    vec = P(("row", "col"))
    return jax.shard_map(
        per_device,
        mesh=mesh,
        in_specs=(spec, spec, vec, vec),
        out_specs=(spec, spec),
        check_vma=False,
    )
```

```python
import jax
import jax.numpy as jnp
import numpy as np
from jax import lax
from jax.experimental import pallas as pl
from jax.experimental.pallas import tpu as pltpu
from jax.sharding import PartitionSpec as P

D = 50
EPSILON_KERNEL = 0.05
SCALE = float(2.0 / (2.0 * D * EPSILON_KERNEL) / np.log(2.0))
EXT = 56
NORM_X, NORM_Y, B_ROW, A_ROW = D, D + 2, D + 4, D + 5
LANES, SUB = 128, 8


f32 = jnp.float32
bf16 = jnp.bfloat16
VM = pl.BlockSpec(memory_space=pltpu.VMEM)
ANY = pl.BlockSpec(memory_space=pl.ANY)


def ext_kernel(x_hbm, y_hbm, a_hbm, b_hbm, o_ref, xv, yv, av, bv, sx, sy, sems):
    copies = [
        pltpu.make_async_copy(src, dst, sems.at[i])
        for i, (src, dst) in enumerate(
            ((x_hbm, xv), (y_hbm, yv), (a_hbm, av), (b_hbm, bv))
        )
    ]
    for c in copies:
        c.start()
    for c in copies:
        c.wait()
    ny = yv.shape[1]
    for src, w, s, norm, one, w_row in (
        (xv, av, sx, NORM_X, NORM_Y, A_ROW),
        (yv, bv, sy, NORM_Y, NORM_X, B_ROW),
    ):
        c = src[...].astype(f32)
        n = -0.5 * jnp.sum(c * c, axis=0, keepdims=True)
        hi = n.astype(bf16).astype(f32)
        s[...] = jnp.zeros_like(s)
        s[0:D, :] = c
        s[norm : norm + 1, :] = hi
        s[norm + 1 : norm + 2, :] = n - hi
        s[one : one + 2, :] = jnp.ones((2, s.shape[1]), f32)
        s[w_row : w_row + 1, :] = w[...].astype(f32).reshape(1, -1)
    o_ref[:, 0:ny] = sy[...].astype(bf16)
    o_ref[:, ny:] = sx[...].astype(bf16)


def kernel_block(xt, y):
    s = lax.dot_general(xt, y, (((1,), (0,)), ((), ())), preferred_element_type=f32)
    return jnp.exp2(s * SCALE)


def add_lanes(acc, e):
    for t in range(e.shape[1] // LANES):
        acc = acc + e[:, t * LANES : (t + 1) * LANES]
    return acc


def make_blocks(xt, ys, ks, acc):
    for n, y in enumerate(ys):
        e = kernel_block(xt[...], y[...])
        if ks:
            ks[n][...] = e
        acc = add_lanes(acc, e)
    return acc


def spread(v, width):
    return jnp.concatenate([v] * (width // LANES), axis=1)


def groups(rows, body, init=0, unroll=8):
    n = rows // SUB

    def step(i, carry):
        return body(pl.ds(pl.multiple_of(i * SUB, SUB), SUB), carry)

    return lax.fori_loop(0, n, step, init, unroll=min(unroll, n))


def row_pass(k, v, acc, unroll):
    def body(rs, carry):
        acc[rs, :] = add_lanes(acc[rs, :], k[rs, :] * v)
        return carry

    groups(k.shape[0], body, unroll=unroll)


def col_pass(k, u, width, unroll):
    def body(rs, carry):
        return carry + k[rs, :] * spread(u[rs, :], width)

    return groups(k.shape[0], body, jnp.zeros((SUB, width), f32), unroll)


def scaling(weights, acc, u):
    u[...] = weights[...] / jnp.broadcast_to(
        jnp.sum(acc[...], axis=1, keepdims=True), u.shape
    )


class Refs:
    def __init__(self, refs):
        self.refs = list(refs)

    def take(self, *counts):
        out = []
        for n in counts:
            out.append(self.refs[:n] if isinstance(n, int) else self.refs[: n[0]][0])
            del self.refs[: n if isinstance(n, int) else n[0]]
        return out


ONE = (1,)


def xor_perm(n, m):
    return [(i, i ^ m) for i in range(n)]


def solution(mesh):
    rows, cols = mesh.shape["row"], mesh.shape["col"]

    def per_device(x_src, y_tgt, a_src, b_tgt):
        nx, ny = x_src.shape[1], y_tgt.shape[1]
        X, T = nx * cols, ny * cols
        kept = X * T * rows * 4 <= 24 * 2**20
        far = list(range(3, rows, 2))
        ends = [0] + far
        width = max(ny, LANES)
        per_row = T // width

        def held(shape, dtype):
            return pltpu.VMEM(shape, dtype) if kept else jax.ShapeDtypeStruct(shape, dtype)

        def call(kernel, outs, args, scratch=(), cost=None, spec=VM):
            return pl.pallas_call(
                kernel,
                out_shape=outs,
                in_specs=[spec] * len(args),
                out_specs=jax.tree.map(lambda _: VM, outs),
                scratch_shapes=scratch,
                compiler_params=pltpu.CompilerParams(vmem_limit_bytes=(4 if kept else 32) * 2**20),
                cost_estimate=cost,
            )(*args)

        def swap(t, m):
            return lax.ppermute(t, "row", xor_perm(rows, m))

        lanes_t = held((X, LANES), f32)
        lanes_s = pltpu.VMEM((X, LANES), f32)
        tot_t = jax.ShapeDtypeStruct((rows, T), f32)
        whole = X // SUB if kept else 8
        n_held = rows if kept else 1 + rows
        spare = [] if kept else [pltpu.VMEM((X, T), f32)]

        def blocks(held_refs, made):
            def get(i):
                if kept:
                    return held_refs[i]
                made[0][...] = kernel_block(held_refs[0][...], held_refs[1 + i][...])
                return made[0]

            return get

        own = call(
            ext_kernel,
            jax.ShapeDtypeStruct((EXT, ny + nx), bf16),
            [
                pltpu.with_memory_space_constraint(t, pltpu.HBM)
                for t in (x_src, y_tgt, a_src, b_tgt)
            ],
            [
                pltpu.VMEM((D, nx), bf16),
                pltpu.VMEM((D, ny), bf16),
                pltpu.VMEM((nx,), bf16),
                pltpu.VMEM((ny,), bf16),
                pltpu.VMEM((EXT, nx), f32),
                pltpu.VMEM((EXT, ny), f32),
                pltpu.SemaphoreType.DMA((4,)),
            ],
            spec=ANY,
        )
        line = [own] + [
            lax.ppermute(own, ("row", "col"), xor_perm(rows * cols, cols + m))
            for m in range(1, cols)
        ]
        both = jnp.concatenate(
            [p[:, 0:ny] for p in line] + [p[:, ny:] for p in line], axis=1
        )
        y0 = both[:, 0:T]
        y, ks = [None] * rows, [None] * rows
        y[0], xe = both[:, 0:T], both[:, T:]

        def start_kernel(e, y_ref, xt, ab, acc, *k):
            xt[...] = jnp.transpose(e[...].astype(f32)).astype(bf16)
            ab[...] = jnp.broadcast_to(xt[:, A_ROW : A_ROW + 1].astype(f32), ab.shape)
            acc[...] = make_blocks(xt, [y_ref], k, jnp.zeros(acc.shape, f32))

        def more_kernel(n, xt, acc, *refs):
            refs[n][...] = make_blocks(xt, refs[:n], refs[n + 1 :], acc[...])

        def more(new, acc):
            cost = pl.CostEstimate(flops=1, bytes_accessed=1, transcendentals=0)
            acc, *k = call(
                lambda *refs: more_kernel(len(new), *refs),
                [lanes_t] + [held((X, T), f32)] * (len(new) * kept),
                [xt, acc] + [y[i] for i in new],
                cost=cost,
            )
            if kept:
                for i, t in zip(new, k):
                    ks[i] = t
            return acc

        raw = {m: swap(y[0], m) for m in range(2, rows, 2)}
        y[1] = swap(y[0], 1)
        xt, ab, acc, *k = call(
            start_kernel,
            [held((X, EXT), bf16), lanes_t, lanes_t] + [held((X, T), f32)] * kept,
            [xe, y[0]],
            cost=pl.CostEstimate(flops=1, bytes_accessed=1, transcendentals=0),
        )
        if kept:
            ks[0] = k[0]
        acc = more([1], acc)
        evens, odds = list(range(2, rows, 2)), list(range(3, rows, 2))
        early, late = evens[:-1], evens[-1:]
        for some in (early, late):
            *lines, acc = lax.optimization_barrier((*[raw[m] for m in some], acc))
            for m, t in zip(some, lines):
                y[m] = t
                y[m + 1] = swap(t, 1)
            acc = more(some, acc)
        acc = more(odds[:-1], acc)
        acc = more(odds[-1:], acc)
        matrix = ks if kept else [xt, *y]

        def column_sums(k, u, tot, unroll):
            for i in range(rows):
                s = col_pass(k(i), u, T, unroll)
                tot[i : i + 1, :] = jnp.sum(s, axis=0, keepdims=True)

        def first_sums(*refs):
            r = Refs(refs)
            acc, ab, kr, tot, u = r.take(ONE, ONE, n_held, ONE, ONE)
            scaling(ab, acc, u)
            column_sums(blocks(kr, r.refs), u, tot, whole)

        tot = call(first_sums, tot_t, [acc, ab, *matrix], [lanes_s] + spare)

        def add_swapped(t, gs, masks):
            def row(i):
                return sum((g[i ^ m : (i ^ m) + 1] for g, m in zip(gs, masks)), t[i : i + 1])

            return jnp.concatenate([row(i) for i in range(rows)], axis=0)

        def add_kernel(t, g, o, send):
            o[...] = add_swapped(t[...], [g[...]], [1])
            send[...] = o[...].astype(bf16)

        tot, send = call(
            add_kernel,
            [tot_t, jax.ShapeDtypeStruct((rows, T), bf16)],
            [tot, swap(tot, 1)],
        )
        got = [swap(send, m) for m in far]

        n_tot = rows * per_row

        def pack_tot(t):
            return jnp.concatenate(
                [t[:, g * width : (g + 1) * width] for g in range(per_row)], axis=0
            ).astype(bf16)

        def unpack_tot(s):
            s = s.astype(f32)
            return jnp.concatenate(
                [s[g * rows : (g + 1) * rows, :] for g in range(per_row)], axis=1
            )

        def second(*refs):
            r = Refs(refs)
            t, gs, ab, x, bs, kr = r.take(ONE, len(far), ONE, ONE, rows, n_held)
            tot_o, keep_o, send_o, acc, u = r.take(ONE, ONE, ONE, ONE, ONE)
            k = blocks(kr, r.refs)
            total = add_swapped(t[...], [g[...].astype(f32) for g in gs], far)
            acc[...] = jnp.zeros_like(acc)
            for i in range(rows):
                v = bs[i][B_ROW : B_ROW + 1, :].astype(f32) / total[i : i + 1, :]
                row_pass(k(i), jnp.broadcast_to(v, (SUB, T)), acc, 32)
            scaling(ab, acc, u)
            column_sums(k, u, tot_o, 32)

            def weighted(mask):
                z = (k(mask)[:, 0:ny] * spread_to(u[...], ny)).astype(bf16)
                return jnp.dot(x[...], z, preferred_element_type=f32)

            send_o[0:n_tot, :] = pack_tot(tot_o[...])
            for n, mask in enumerate(ends):
                keep_o[n, :, 0:ny] = weighted(mask)
                at = n_tot + n * EXT
                send_o[at : at + EXT, 0:ny] = weighted(mask ^ 1).astype(bf16)

        def spread_to(u, n):
            return u[:, 0:n] if n <= LANES else spread(u, n)

        tot, keep, send = call(
            second,
            (
                tot_t,
                jax.ShapeDtypeStruct((len(ends), EXT, width), f32),
                jax.ShapeDtypeStruct((n_tot + len(ends) * EXT, width), bf16),
            ),
            [tot, *got, ab, xe, *y, *matrix],
            [lanes_s] * 2 + spare,
        )

        def join(t, kp, g, tot_o, keep_o, *sends):
            tot_o[...] = add_swapped(t[...], [unpack_tot(g[0:n_tot, :])], [1])
            packed = pack_tot(tot_o[...])
            for n in range(len(ends)):
                s = kp[n] + g[n_tot + n * EXT : n_tot + (n + 1) * EXT, :].astype(f32)
                if n == 0:
                    keep_o[...] = s
                else:
                    sends[n - 1][0:n_tot, :] = packed
                    sends[n - 1][n_tot:, :] = s.astype(bf16)

        tot, keep, *send = call(
            join,
            [tot_t, jax.ShapeDtypeStruct((EXT, width), f32)]
            + [jax.ShapeDtypeStruct((n_tot + EXT, width), bf16)] * len(far),
            [tot, keep, swap(send, 1)],
        )
        got = [swap(t, m) for t, m in zip(send, far)]

        def final(*refs):
            r = Refs(refs)
            t, kp, gs, xt, ys = r.take(ONE, ONE, len(far), ONE, rows)
            kr, src_o, tgt_o = r.take(rows * kept, ONE, ONE)
            total = add_swapped(t[...], [unpack_tot(g[0:n_tot, :]) for g in gs], far)
            num = sum((g[n_tot:, :].astype(f32) for g in gs), kp[...])
            tgt_o[...] = num[0:D, 0:ny] / total[0:1, 0:ny]
            res = jnp.zeros((nx, EXT), f32)
            for i in range(rows):
                yi = ys[i][...]
                v = yi[B_ROW : B_ROW + 1, :].astype(f32) / total[i : i + 1, :]
                e = kr[i][0:nx, :] if kept else kernel_block(xt[0:nx, :], yi)
                res = res + lax.dot_general(
                    (e * v).astype(bf16),
                    yi,
                    (((1,), (1,)), ((), ())),
                    preferred_element_type=f32,
                )
            res = jnp.transpose(res)
            src_o[...] = res[0:D, :] / res[NORM_X : NORM_X + 1, :]

        return tuple(
            call(
                final,
                (
                    jax.ShapeDtypeStruct((D, nx), f32),
                    jax.ShapeDtypeStruct((D, ny), f32),
                ),
                [tot, keep, *got, xt, *y, *(ks if kept else [])],
            )
        )

    spec = P(None, ("row", "col"))
    vec = P(("row", "col"))
    return jax.shard_map(
        per_device,
        mesh=mesh,
        in_specs=(spec, spec, vec, vec),
        out_specs=(spec, spec),
        check_vma=False,
    )
```

```python
import jax
import jax.numpy as jnp
import numpy as np
from jax import lax
from jax.experimental import pallas as pl
from jax.experimental.pallas import tpu as pltpu
from jax.sharding import PartitionSpec as P

D = 50
EPSILON_KERNEL = 0.05
SCALE = float(2.0 / (2.0 * D * EPSILON_KERNEL) / np.log(2.0))
EXT = 56
NORM_X, NORM_Y, B_ROW, A_ROW = D, D + 2, D + 4, D + 5
LANES, SUB = 128, 8


f32 = jnp.float32
bf16 = jnp.bfloat16
VM = pl.BlockSpec(memory_space=pltpu.VMEM)
ANY = pl.BlockSpec(memory_space=pl.ANY)


def ext_kernel(x_hbm, y_hbm, a_hbm, b_hbm, o_ref, xv, yv, av, bv, sx, sy, sems):
    copies = [
        pltpu.make_async_copy(src, dst, sems.at[i])
        for i, (src, dst) in enumerate(
            ((x_hbm, xv), (y_hbm, yv), (a_hbm, av), (b_hbm, bv))
        )
    ]
    for c in copies:
        c.start()
    for c in copies:
        c.wait()
    ny = yv.shape[1]
    for src, w, s, norm, one, w_row in (
        (xv, av, sx, NORM_X, NORM_Y, A_ROW),
        (yv, bv, sy, NORM_Y, NORM_X, B_ROW),
    ):
        c = src[...].astype(f32)
        n = -0.5 * jnp.sum(c * c, axis=0, keepdims=True)
        hi = n.astype(bf16).astype(f32)
        s[...] = jnp.zeros_like(s)
        s[0:D, :] = c
        s[norm : norm + 1, :] = hi
        s[norm + 1 : norm + 2, :] = n - hi
        s[one : one + 2, :] = jnp.ones((2, s.shape[1]), f32)
        s[w_row : w_row + 1, :] = w[...].astype(f32).reshape(1, -1)
    o_ref[:, 0:ny] = sy[...].astype(bf16)
    o_ref[:, ny:] = sx[...].astype(bf16)


def kernel_block(xt, y):
    s = lax.dot_general(xt, y, (((1,), (0,)), ((), ())), preferred_element_type=f32)
    return jnp.exp2(s * SCALE)


def add_lanes(acc, e):
    for t in range(e.shape[1] // LANES):
        acc = acc + e[:, t * LANES : (t + 1) * LANES]
    return acc


def make_blocks(xt, ys, ks, acc):
    for n, y in enumerate(ys):
        e = kernel_block(xt[...], y[...])
        if ks:
            ks[n][...] = e
        acc = add_lanes(acc, e)
    return acc


def spread(v, width):
    return jnp.concatenate([v] * (width // LANES), axis=1)


def groups(rows, body, init=0, unroll=8):
    n = rows // SUB

    def step(i, carry):
        return body(pl.ds(pl.multiple_of(i * SUB, SUB), SUB), carry)

    return lax.fori_loop(0, n, step, init, unroll=min(unroll, n))


def row_pass(k, v, acc, unroll):
    def body(rs, carry):
        acc[rs, :] = add_lanes(acc[rs, :], k[rs, :] * v)
        return carry

    groups(k.shape[0], body, unroll=unroll)


def col_pass(k, u, width, unroll):
    def body(rs, carry):
        return carry + k[rs, :] * spread(u[rs, :], width)

    return groups(k.shape[0], body, jnp.zeros((SUB, width), f32), unroll)


def scaling(weights, acc, u):
    u[...] = weights[...] / jnp.broadcast_to(
        jnp.sum(acc[...], axis=1, keepdims=True), u.shape
    )


class Refs:
    def __init__(self, refs):
        self.refs = list(refs)

    def take(self, *counts):
        out = []
        for n in counts:
            out.append(self.refs[:n] if isinstance(n, int) else self.refs[: n[0]][0])
            del self.refs[: n if isinstance(n, int) else n[0]]
        return out


ONE = (1,)


def xor_perm(n, m):
    return [(i, i ^ m) for i in range(n)]


def solution(mesh):
    rows, cols = mesh.shape["row"], mesh.shape["col"]

    def per_device(x_src, y_tgt, a_src, b_tgt):
        nx, ny = x_src.shape[1], y_tgt.shape[1]
        X, T = nx * cols, ny * cols
        kept = X * T * rows * 4 <= 24 * 2**20
        far = list(range(3, rows, 2))
        ends = [0] + far
        width = max(ny, LANES)
        per_row = T // width

        def held(shape, dtype):
            return pltpu.VMEM(shape, dtype) if kept else jax.ShapeDtypeStruct(shape, dtype)

        def call(kernel, outs, args, scratch=(), cost=None, spec=VM):
            return pl.pallas_call(
                kernel,
                out_shape=outs,
                in_specs=[spec] * len(args),
                out_specs=jax.tree.map(lambda _: VM, outs),
                scratch_shapes=scratch,
                compiler_params=pltpu.CompilerParams(vmem_limit_bytes=(4 if kept else 32) * 2**20),
                cost_estimate=cost,
            )(*args)

        def swap(t, m):
            return lax.ppermute(t, "row", xor_perm(rows, m))

        lanes_t = held((X, LANES), f32)
        lanes_s = pltpu.VMEM((X, LANES), f32)
        tot_t = jax.ShapeDtypeStruct((rows, T), f32)
        whole = X // SUB if kept else 8
        n_held = rows if kept else 1 + rows
        spare = [] if kept else [pltpu.VMEM((X, T), f32)]

        def blocks(held_refs, made):
            def get(i):
                if kept:
                    return held_refs[i]
                made[0][...] = kernel_block(held_refs[0][...], held_refs[1 + i][...])
                return made[0]

            return get

        own = call(
            ext_kernel,
            jax.ShapeDtypeStruct((EXT, ny + nx), bf16),
            [
                pltpu.with_memory_space_constraint(t, pltpu.HBM)
                for t in (x_src, y_tgt, a_src, b_tgt)
            ],
            [
                pltpu.VMEM((D, nx), bf16),
                pltpu.VMEM((D, ny), bf16),
                pltpu.VMEM((nx,), bf16),
                pltpu.VMEM((ny,), bf16),
                pltpu.VMEM((EXT, nx), f32),
                pltpu.VMEM((EXT, ny), f32),
                pltpu.SemaphoreType.DMA((4,)),
            ],
            spec=ANY,
        )
        line = [own] + [
            lax.ppermute(own, ("row", "col"), xor_perm(rows * cols, cols + m))
            for m in range(1, cols)
        ]
        both = jnp.concatenate(
            [p[:, 0:ny] for p in line] + [p[:, ny:] for p in line], axis=1
        )
        y0 = both[:, 0:T]
        y, ks = [None] * rows, [None] * rows
        y[0], xe = both[:, 0:T], both[:, T:]

        def start_kernel(e, y_ref, xt, ab, acc, *k):
            xt[...] = jnp.transpose(e[...].astype(f32)).astype(bf16)
            ab[...] = jnp.broadcast_to(xt[:, A_ROW : A_ROW + 1].astype(f32), ab.shape)
            acc[...] = make_blocks(xt, [y_ref], k, jnp.zeros(acc.shape, f32))

        def more_kernel(n, xt, acc, *refs):
            refs[n][...] = make_blocks(xt, refs[:n], refs[n + 1 :], acc[...])

        def more(new, acc):
            cost = pl.CostEstimate(flops=1, bytes_accessed=1, transcendentals=0)
            acc, *k = call(
                lambda *refs: more_kernel(len(new), *refs),
                [lanes_t] + [held((X, T), f32)] * (len(new) * kept),
                [xt, acc] + [y[i] for i in new],
                cost=cost,
            )
            if kept:
                for i, t in zip(new, k):
                    ks[i] = t
            return acc

        raw = {m: swap(y[0], m) for m in range(2, rows, 2)}
        y[1] = swap(y[0], 1)
        xt, ab, acc, *k = call(
            start_kernel,
            [held((X, EXT), bf16), lanes_t, lanes_t] + [held((X, T), f32)] * kept,
            [xe, y[0]],
            cost=pl.CostEstimate(flops=1, bytes_accessed=1, transcendentals=0),
        )
        if kept:
            ks[0] = k[0]
        acc = more([1], acc)
        evens, odds = list(range(2, rows, 2)), list(range(3, rows, 2))
        early, late = evens[:-1], evens[-1:]
        for some in (early, late):
            *lines, acc = lax.optimization_barrier((*[raw[m] for m in some], acc))
            for m, t in zip(some, lines):
                y[m] = t
                y[m + 1] = swap(t, 1)
            acc = more(some, acc)
        acc = more(odds[:-1], acc)
        acc = more(odds[-1:], acc)
        matrix = ks if kept else [xt, *y]

        def column_sums(k, u, tot, unroll):
            for i in range(rows):
                s = col_pass(k(i), u, T, unroll)
                tot[i : i + 1, :] = jnp.sum(s, axis=0, keepdims=True)

        def first_sums(*refs):
            r = Refs(refs)
            acc, ab, kr, tot, u = r.take(ONE, ONE, n_held, ONE, ONE)
            scaling(ab, acc, u)
            column_sums(blocks(kr, r.refs), u, tot, whole)

        tot = call(first_sums, tot_t, [acc, ab, *matrix], [lanes_s] + spare)

        def add_swapped(t, gs, masks):
            def row(i):
                return sum((g[i ^ m : (i ^ m) + 1] for g, m in zip(gs, masks)), t[i : i + 1])

            return jnp.concatenate([row(i) for i in range(rows)], axis=0)

        def add_kernel(t, g, o, send):
            o[...] = add_swapped(t[...], [g[...]], [1])
            send[...] = o[...].astype(bf16)

        tot, send = call(
            add_kernel,
            [tot_t, jax.ShapeDtypeStruct((rows, T), bf16)],
            [tot, swap(tot, 1)],
        )
        got = [swap(send, m) for m in far]

        n_tot = rows * per_row

        def pack_tot(t):
            return jnp.concatenate(
                [t[:, g * width : (g + 1) * width] for g in range(per_row)], axis=0
            ).astype(bf16)

        def unpack_tot(s):
            s = s.astype(f32)
            return jnp.concatenate(
                [s[g * rows : (g + 1) * rows, :] for g in range(per_row)], axis=1
            )

        def second_rows(*refs):
            r = Refs(refs)
            t, gs, ab, bs, kr = r.take(ONE, len(far), ONE, rows, n_held)
            u, acc = r.take(ONE, ONE)
            k = blocks(kr, r.refs)
            total = add_swapped(t[...], [g[...].astype(f32) for g in gs], far)
            acc[...] = jnp.zeros_like(acc)
            for i in range(rows):
                v = bs[i][B_ROW : B_ROW + 1, :].astype(f32) / total[i : i + 1, :]
                row_pass(k(i), jnp.broadcast_to(v, (SUB, T)), acc, 64)
            scaling(ab, acc, u)

        u = call(
            second_rows,
            lanes_t,
            [tot, *got, ab, *y, *matrix],
            [lanes_s] + spare,
        )

        def second_cols(*refs):
            r = Refs(refs)
            u, x, kr = r.take(ONE, ONE, n_held)
            tot_o, keep_o, send_o = r.take(ONE, ONE, ONE)
            k = blocks(kr, r.refs)
            column_sums(k, u, tot_o, 64)

            def weighted(mask):
                z = (k(mask)[:, 0:ny] * spread_to(u[...], ny)).astype(bf16)
                return jnp.dot(x[...], z, preferred_element_type=f32)

            send_o[0:n_tot, :] = pack_tot(tot_o[...])
            for n, mask in enumerate(ends):
                keep_o[n, :, 0:ny] = weighted(mask)
                at = n_tot + n * EXT
                send_o[at : at + EXT, 0:ny] = weighted(mask ^ 1).astype(bf16)

        def spread_to(u, n):
            return u[:, 0:n] if n <= LANES else spread(u, n)

        tot, keep, send = call(
            second_cols,
            (
                tot_t,
                jax.ShapeDtypeStruct((len(ends), EXT, width), f32),
                jax.ShapeDtypeStruct((n_tot + len(ends) * EXT, width), bf16),
            ),
            [u, xe, *matrix],
            spare,
        )

        def join(t, kp, g, tot_o, keep_o, *sends):
            tot_o[...] = add_swapped(t[...], [unpack_tot(g[0:n_tot, :])], [1])
            packed = pack_tot(tot_o[...])
            for n in range(len(ends)):
                s = kp[n] + g[n_tot + n * EXT : n_tot + (n + 1) * EXT, :].astype(f32)
                if n == 0:
                    keep_o[...] = s
                else:
                    sends[n - 1][0:n_tot, :] = packed
                    sends[n - 1][n_tot:, :] = s.astype(bf16)

        tot, keep, *send = call(
            join,
            [tot_t, jax.ShapeDtypeStruct((EXT, width), f32)]
            + [jax.ShapeDtypeStruct((n_tot + EXT, width), bf16)] * len(far),
            [tot, keep, swap(send, 1)],
        )
        got = [swap(t, m) for t, m in zip(send, far)]

        def final(*refs):
            r = Refs(refs)
            t, kp, gs, xt, ys = r.take(ONE, ONE, len(far), ONE, rows)
            kr, src_o, tgt_o = r.take(rows * kept, ONE, ONE)
            total = add_swapped(t[...], [unpack_tot(g[0:n_tot, :]) for g in gs], far)
            num = sum((g[n_tot:, :].astype(f32) for g in gs), kp[...])
            tgt_o[...] = num[0:D, 0:ny] / total[0:1, 0:ny]
            res = jnp.zeros((nx, EXT), f32)
            for i in range(rows):
                yi = ys[i][...]
                v = yi[B_ROW : B_ROW + 1, :].astype(f32) / total[i : i + 1, :]
                e = kr[i][0:nx, :] if kept else kernel_block(xt[0:nx, :], yi)
                res = res + lax.dot_general(
                    (e * v).astype(bf16),
                    yi,
                    (((1,), (1,)), ((), ())),
                    preferred_element_type=f32,
                )
            res = jnp.transpose(res)
            src_o[...] = res[0:D, :] / res[NORM_X : NORM_X + 1, :]

        return tuple(
            call(
                final,
                (
                    jax.ShapeDtypeStruct((D, nx), f32),
                    jax.ShapeDtypeStruct((D, ny), f32),
                ),
                [tot, keep, *got, xt, *y, *(ks if kept else [])],
            )
        )

    spec = P(None, ("row", "col"))
    vec = P(("row", "col"))
    return jax.shard_map(
        per_device,
        mesh=mesh,
        in_specs=(spec, spec, vec, vec),
        out_specs=(spec, spec),
        check_vma=False,
    )
```

```python
import jax
import jax.numpy as jnp
import numpy as np
from jax import lax
from jax.experimental import pallas as pl
from jax.experimental.pallas import tpu as pltpu
from jax.sharding import PartitionSpec as P

D = 50
EPSILON_KERNEL = 0.05
SCALE = float(2.0 / (2.0 * D * EPSILON_KERNEL) / np.log(2.0))
EXT = 56
NORM_X, NORM_Y, B_ROW, A_ROW = D, D + 2, D + 4, D + 5
LANES, SUB = 128, 8


f32 = jnp.float32
bf16 = jnp.bfloat16
VM = pl.BlockSpec(memory_space=pltpu.VMEM)
ANY = pl.BlockSpec(memory_space=pl.ANY)


def ext_kernel(x_hbm, y_hbm, a_hbm, b_hbm, o_ref, xv, yv, av, bv, sx, sy, sems):
    copies = [
        pltpu.make_async_copy(src, dst, sems.at[i])
        for i, (src, dst) in enumerate(
            ((x_hbm, xv), (y_hbm, yv), (a_hbm, av), (b_hbm, bv))
        )
    ]
    for c in copies:
        c.start()
    for c in copies:
        c.wait()
    ny = yv.shape[1]
    for src, w, s, norm, one, w_row in (
        (xv, av, sx, NORM_X, NORM_Y, A_ROW),
        (yv, bv, sy, NORM_Y, NORM_X, B_ROW),
    ):
        c = src[...].astype(f32)
        n = -0.5 * jnp.sum(c * c, axis=0, keepdims=True)
        hi = n.astype(bf16).astype(f32)
        s[...] = jnp.zeros_like(s)
        s[0:D, :] = c
        s[norm : norm + 1, :] = hi
        s[norm + 1 : norm + 2, :] = n - hi
        s[one : one + 2, :] = jnp.ones((2, s.shape[1]), f32)
        s[w_row : w_row + 1, :] = w[...].astype(f32).reshape(1, -1)
    o_ref[:, 0:ny] = sy[...].astype(bf16)
    o_ref[:, ny:] = sx[...].astype(bf16)


def kernel_block(xt, y):
    s = lax.dot_general(xt, y, (((1,), (0,)), ((), ())), preferred_element_type=f32)
    return jnp.exp2(s * SCALE)


def add_lanes(acc, e):
    for t in range(e.shape[1] // LANES):
        acc = acc + e[:, t * LANES : (t + 1) * LANES]
    return acc


def make_blocks(xt, ys, ks, acc):
    for n, y in enumerate(ys):
        e = kernel_block(xt[...], y[...])
        if ks:
            ks[n][...] = e
        acc = add_lanes(acc, e)
    return acc


def spread(v, width):
    return jnp.concatenate([v] * (width // LANES), axis=1)


def groups(rows, body, init=0, unroll=8):
    n = rows // SUB

    def step(i, carry):
        return body(pl.ds(pl.multiple_of(i * SUB, SUB), SUB), carry)

    return lax.fori_loop(0, n, step, init, unroll=min(unroll, n))


def row_pass(k, v, acc, unroll):
    def body(rs, carry):
        acc[rs, :] = add_lanes(acc[rs, :], k[rs, :] * v)
        return carry

    groups(k.shape[0], body, unroll=unroll)


def col_pass(k, u, width, unroll):
    def body(rs, carry):
        return carry + k[rs, :] * spread(u[rs, :], width)

    return groups(k.shape[0], body, jnp.zeros((SUB, width), f32), unroll)


def scaling(weights, acc, u):
    u[...] = weights[...] / jnp.broadcast_to(
        jnp.sum(acc[...], axis=1, keepdims=True), u.shape
    )


class Refs:
    def __init__(self, refs):
        self.refs = list(refs)

    def take(self, *counts):
        out = []
        for n in counts:
            out.append(self.refs[:n] if isinstance(n, int) else self.refs[: n[0]][0])
            del self.refs[: n if isinstance(n, int) else n[0]]
        return out


ONE = (1,)


def xor_perm(n, m):
    return [(i, i ^ m) for i in range(n)]


def solution(mesh):
    rows, cols = mesh.shape["row"], mesh.shape["col"]

    def per_device(x_src, y_tgt, a_src, b_tgt):
        nx, ny = x_src.shape[1], y_tgt.shape[1]
        X, T = nx * cols, ny * cols
        kept = X * T * rows * 4 <= 24 * 2**20
        far = list(range(3, rows, 2))
        ends = [0] + far
        width = max(ny, LANES)
        per_row = T // width

        def held(shape, dtype):
            return pltpu.VMEM(shape, dtype) if kept else jax.ShapeDtypeStruct(shape, dtype)

        def call(kernel, outs, args, scratch=(), cost=None, spec=VM):
            return pl.pallas_call(
                kernel,
                out_shape=outs,
                in_specs=[spec] * len(args),
                out_specs=jax.tree.map(lambda _: VM, outs),
                scratch_shapes=scratch,
                compiler_params=pltpu.CompilerParams(vmem_limit_bytes=(4 if kept else 32) * 2**20),
                cost_estimate=cost,
            )(*args)

        def swap(t, m):
            return lax.ppermute(t, "row", xor_perm(rows, m))

        lanes_t = held((X, LANES), f32)
        lanes_s = pltpu.VMEM((X, LANES), f32)
        tot_t = jax.ShapeDtypeStruct((rows, T), f32)
        whole = X // SUB if kept else 8
        n_held = rows if kept else 1 + rows
        spare = [] if kept else [pltpu.VMEM((X, T), f32)]

        def blocks(held_refs, made):
            def get(i):
                if kept:
                    return held_refs[i]
                made[0][...] = kernel_block(held_refs[0][...], held_refs[1 + i][...])
                return made[0]

            return get

        own = call(
            ext_kernel,
            jax.ShapeDtypeStruct((EXT, ny + nx), bf16),
            [
                pltpu.with_memory_space_constraint(t, pltpu.HBM)
                for t in (x_src, y_tgt, a_src, b_tgt)
            ],
            [
                pltpu.VMEM((D, nx), bf16),
                pltpu.VMEM((D, ny), bf16),
                pltpu.VMEM((nx,), bf16),
                pltpu.VMEM((ny,), bf16),
                pltpu.VMEM((EXT, nx), f32),
                pltpu.VMEM((EXT, ny), f32),
                pltpu.SemaphoreType.DMA((4,)),
            ],
            spec=ANY,
        )
        line = [own] + [
            lax.ppermute(own, ("row", "col"), xor_perm(rows * cols, cols + m))
            for m in range(1, cols)
        ]
        both = jnp.concatenate(
            [p[:, 0:ny] for p in line] + [p[:, ny:] for p in line], axis=1
        )
        y0 = both[:, 0:T]
        y, ks = [None] * rows, [None] * rows
        y[0], xe = both[:, 0:T], both[:, T:]

        def start_kernel(e, y_ref, xt, ab, acc, *k):
            xt[...] = jnp.transpose(e[...].astype(f32)).astype(bf16)
            ab[...] = jnp.broadcast_to(xt[:, A_ROW : A_ROW + 1].astype(f32), ab.shape)
            acc[...] = make_blocks(xt, [y_ref], k, jnp.zeros(acc.shape, f32))

        def more_kernel(n, xt, acc, *refs):
            refs[n][...] = make_blocks(xt, refs[:n], refs[n + 1 :], acc[...])

        def more(new, acc):
            cost = pl.CostEstimate(flops=1, bytes_accessed=1, transcendentals=0)
            acc, *k = call(
                lambda *refs: more_kernel(len(new), *refs),
                [lanes_t] + [held((X, T), f32)] * (len(new) * kept),
                [xt, acc] + [y[i] for i in new],
                cost=cost,
            )
            if kept:
                for i, t in zip(new, k):
                    ks[i] = t
            return acc

        raw = {m: swap(y[0], m) for m in (*range(2, rows - 2, 2), rows - 1)}
        y[1] = swap(y[0], 1)
        xt, ab, acc, *k = call(
            start_kernel,
            [held((X, EXT), bf16), lanes_t, lanes_t] + [held((X, T), f32)] * kept,
            [xe, y[0]],
            cost=pl.CostEstimate(flops=1, bytes_accessed=1, transcendentals=0),
        )
        if kept:
            ks[0] = k[0]
        acc = more([1], acc)
        early, late = list(raw)[:-1], list(raw)[-1:]
        for some, others in ((early, []), (late, [m ^ 1 for m in early])):
            *lines, acc = lax.optimization_barrier((*[raw[m] for m in some], acc))
            for m, t in zip(some, lines):
                y[m] = t
                y[m ^ 1] = swap(t, 1)
            acc = more(some + others, acc)
        acc = more([m ^ 1 for m in late], acc)
        matrix = ks if kept else [xt, *y]

        def column_sums(k, u, tot, unroll):
            for i in range(rows):
                s = col_pass(k(i), u, T, unroll)
                tot[i : i + 1, :] = jnp.sum(s, axis=0, keepdims=True)

        def first_sums(*refs):
            r = Refs(refs)
            acc, ab, kr, tot, u = r.take(ONE, ONE, n_held, ONE, ONE)
            scaling(ab, acc, u)
            column_sums(blocks(kr, r.refs), u, tot, whole)

        tot = call(first_sums, tot_t, [acc, ab, *matrix], [lanes_s] + spare)

        def add_swapped(t, gs, masks):
            def row(i):
                return sum((g[i ^ m : (i ^ m) + 1] for g, m in zip(gs, masks)), t[i : i + 1])

            return jnp.concatenate([row(i) for i in range(rows)], axis=0)

        def add_kernel(t, g, o, send):
            o[...] = add_swapped(t[...], [g[...]], [1])
            send[...] = o[...].astype(bf16)

        tot, send = call(
            add_kernel,
            [tot_t, jax.ShapeDtypeStruct((rows, T), bf16)],
            [tot, swap(tot, 1)],
        )
        got = [swap(send, m) for m in far]

        n_tot = rows * per_row

        def pack_tot(t):
            return jnp.concatenate(
                [t[:, g * width : (g + 1) * width] for g in range(per_row)], axis=0
            ).astype(bf16)

        def unpack_tot(s):
            s = s.astype(f32)
            return jnp.concatenate(
                [s[g * rows : (g + 1) * rows, :] for g in range(per_row)], axis=1
            )

        def second_rows(*refs):
            r = Refs(refs)
            t, gs, ab, bs, kr = r.take(ONE, len(far), ONE, rows, n_held)
            u, acc = r.take(ONE, ONE)
            k = blocks(kr, r.refs)
            total = add_swapped(t[...], [g[...].astype(f32) for g in gs], far)
            acc[...] = jnp.zeros_like(acc)
            for i in range(rows):
                v = bs[i][B_ROW : B_ROW + 1, :].astype(f32) / total[i : i + 1, :]
                row_pass(k(i), jnp.broadcast_to(v, (SUB, T)), acc, 64)
            scaling(ab, acc, u)

        u = call(
            second_rows,
            lanes_t,
            [tot, *got, ab, *y, *matrix],
            [lanes_s] + spare,
        )

        def second_cols(*refs):
            r = Refs(refs)
            u, x, kr = r.take(ONE, ONE, n_held)
            tot_o, keep_o, send_o = r.take(ONE, ONE, ONE)
            k = blocks(kr, r.refs)
            column_sums(k, u, tot_o, 64)

            def weighted(mask):
                z = (k(mask)[:, 0:ny] * spread_to(u[...], ny)).astype(bf16)
                return jnp.dot(x[...], z, preferred_element_type=f32)

            send_o[0:n_tot, :] = pack_tot(tot_o[...])
            for n, mask in enumerate(ends):
                keep_o[n, :, 0:ny] = weighted(mask)
                at = n_tot + n * EXT
                send_o[at : at + EXT, 0:ny] = weighted(mask ^ 1).astype(bf16)

        def spread_to(u, n):
            return u[:, 0:n] if n <= LANES else spread(u, n)

        tot, keep, send = call(
            second_cols,
            (
                tot_t,
                jax.ShapeDtypeStruct((len(ends), EXT, width), f32),
                jax.ShapeDtypeStruct((n_tot + len(ends) * EXT, width), bf16),
            ),
            [u, xe, *matrix],
            spare,
        )

        def join(t, kp, g, tot_o, keep_o, *sends):
            tot_o[...] = add_swapped(t[...], [unpack_tot(g[0:n_tot, :])], [1])
            packed = pack_tot(tot_o[...])
            for n in range(len(ends)):
                s = kp[n] + g[n_tot + n * EXT : n_tot + (n + 1) * EXT, :].astype(f32)
                if n == 0:
                    keep_o[...] = s
                else:
                    sends[n - 1][0:n_tot, :] = packed
                    sends[n - 1][n_tot:, :] = s.astype(bf16)

        tot, keep, *send = call(
            join,
            [tot_t, jax.ShapeDtypeStruct((EXT, width), f32)]
            + [jax.ShapeDtypeStruct((n_tot + EXT, width), bf16)] * len(far),
            [tot, keep, swap(send, 1)],
        )
        got = [swap(t, m) for t, m in zip(send, far)]

        def final(*refs):
            r = Refs(refs)
            t, kp, gs, xt, ys = r.take(ONE, ONE, len(far), ONE, rows)
            kr, src_o, tgt_o = r.take(rows * kept, ONE, ONE)
            total = add_swapped(t[...], [unpack_tot(g[0:n_tot, :]) for g in gs], far)
            num = sum((g[n_tot:, :].astype(f32) for g in gs), kp[...])
            tgt_o[...] = num[0:D, 0:ny] / total[0:1, 0:ny]
            res = jnp.zeros((nx, EXT), f32)
            for i in range(rows):
                yi = ys[i][...]
                v = yi[B_ROW : B_ROW + 1, :].astype(f32) / total[i : i + 1, :]
                e = kr[i][0:nx, :] if kept else kernel_block(xt[0:nx, :], yi)
                res = res + lax.dot_general(
                    (e * v).astype(bf16),
                    yi,
                    (((1,), (1,)), ((), ())),
                    preferred_element_type=f32,
                )
            res = jnp.transpose(res)
            src_o[...] = res[0:D, :] / res[NORM_X : NORM_X + 1, :]

        return tuple(
            call(
                final,
                (
                    jax.ShapeDtypeStruct((D, nx), f32),
                    jax.ShapeDtypeStruct((D, ny), f32),
                ),
                [tot, keep, *got, xt, *y, *(ks if kept else [])],
            )
        )

    spec = P(None, ("row", "col"))
    vec = P(("row", "col"))
    return jax.shard_map(
        per_device,
        mesh=mesh,
        in_specs=(spec, spec, vec, vec),
        out_specs=(spec, spec),
        check_vma=False,
    )
```

```python
import jax
import jax.numpy as jnp
import numpy as np
from jax import lax
from jax.experimental import pallas as pl
from jax.experimental.pallas import tpu as pltpu
from jax.sharding import PartitionSpec as P

D = 50
EPSILON_KERNEL = 0.05
SCALE = float(2.0 / (2.0 * D * EPSILON_KERNEL) / np.log(2.0))
EXT = 56
NORM_X, NORM_Y, B_ROW, A_ROW = D, D + 2, D + 4, D + 5
LANES, SUB = 128, 8


f32 = jnp.float32
bf16 = jnp.bfloat16
VM = pl.BlockSpec(memory_space=pltpu.VMEM)
ANY = pl.BlockSpec(memory_space=pl.ANY)


def ext_kernel(x_hbm, y_hbm, a_hbm, b_hbm, o_ref, xv, yv, av, bv, sx, sy, sems):
    copies = [
        pltpu.make_async_copy(src, dst, sems.at[i])
        for i, (src, dst) in enumerate(
            ((x_hbm, xv), (y_hbm, yv), (a_hbm, av), (b_hbm, bv))
        )
    ]
    for c in copies:
        c.start()
    for c in copies:
        c.wait()
    ny = yv.shape[1]
    for src, w, s, norm, one, w_row in (
        (xv, av, sx, NORM_X, NORM_Y, A_ROW),
        (yv, bv, sy, NORM_Y, NORM_X, B_ROW),
    ):
        c = src[...].astype(f32)
        n = -0.5 * jnp.sum(c * c, axis=0, keepdims=True)
        hi = n.astype(bf16).astype(f32)
        s[...] = jnp.zeros_like(s)
        s[0:D, :] = c
        s[norm : norm + 1, :] = hi
        s[norm + 1 : norm + 2, :] = n - hi
        s[one : one + 2, :] = jnp.ones((2, s.shape[1]), f32)
        s[w_row : w_row + 1, :] = w[...].astype(f32).reshape(1, -1)
    o_ref[:, 0:ny] = sy[...].astype(bf16)
    o_ref[:, ny:] = sx[...].astype(bf16)


def kernel_block(xt, y):
    s = lax.dot_general(xt, y, (((1,), (0,)), ((), ())), preferred_element_type=f32)
    return jnp.exp2(s * SCALE)


def add_lanes(acc, e):
    for t in range(e.shape[1] // LANES):
        acc = acc + e[:, t * LANES : (t + 1) * LANES]
    return acc


def make_blocks(xt, ys, ks, acc):
    for n, y in enumerate(ys):
        e = kernel_block(xt[...], y[...])
        if ks:
            ks[n][...] = e
        acc = add_lanes(acc, e)
    return acc


def spread(v, width):
    return jnp.concatenate([v] * (width // LANES), axis=1)


def groups(rows, body, init=0, unroll=8):
    n = rows // SUB

    def step(i, carry):
        return body(pl.ds(pl.multiple_of(i * SUB, SUB), SUB), carry)

    return lax.fori_loop(0, n, step, init, unroll=min(unroll, n))


def row_pass(k, v, acc, unroll):
    def body(rs, carry):
        acc[rs, :] = add_lanes(acc[rs, :], k[rs, :] * v)
        return carry

    groups(k.shape[0], body, unroll=unroll)


def col_pass(k, u, width, unroll, z=None):
    step = 2 * SUB

    def body(i, carry):
        rs = pl.ds(pl.multiple_of(i * step, step), step)
        p = k[rs, :] * spread(u[rs, :], width)
        if z is not None:
            z[rs, :] = p[:, 0 : z.shape[1]].astype(bf16)
        return carry + p[0:SUB, :] + p[SUB:, :]

    n = k.shape[0] // step
    return lax.fori_loop(
        0, n, body, jnp.zeros((SUB, width), f32), unroll=min(unroll // 2, n)
    )


def scaling(weights, acc, u):
    u[...] = weights[...] / jnp.broadcast_to(
        jnp.sum(acc[...], axis=1, keepdims=True), u.shape
    )


class Refs:
    def __init__(self, refs):
        self.refs = list(refs)

    def take(self, *counts):
        out = []
        for n in counts:
            out.append(self.refs[:n] if isinstance(n, int) else self.refs[: n[0]][0])
            del self.refs[: n if isinstance(n, int) else n[0]]
        return out


ONE = (1,)


def xor_perm(n, m):
    return [(i, i ^ m) for i in range(n)]


def solution(mesh):
    rows, cols = mesh.shape["row"], mesh.shape["col"]

    def per_device(x_src, y_tgt, a_src, b_tgt):
        nx, ny = x_src.shape[1], y_tgt.shape[1]
        X, T = nx * cols, ny * cols
        kept = X * T * rows * 4 <= 24 * 2**20
        far = list(range(3, rows, 2))
        ends = [0] + far
        width = max(ny, LANES)
        per_row = T // width

        def held(shape, dtype):
            return pltpu.VMEM(shape, dtype) if kept else jax.ShapeDtypeStruct(shape, dtype)

        def call(kernel, outs, args, scratch=(), cost=None, spec=VM):
            return pl.pallas_call(
                kernel,
                out_shape=outs,
                in_specs=[spec] * len(args),
                out_specs=jax.tree.map(lambda _: VM, outs),
                scratch_shapes=scratch,
                compiler_params=pltpu.CompilerParams(vmem_limit_bytes=(4 if kept else 32) * 2**20),
                cost_estimate=cost,
            )(*args)

        def swap(t, m):
            return lax.ppermute(t, "row", xor_perm(rows, m))

        lanes_t = held((X, LANES), f32)
        lanes_s = pltpu.VMEM((X, LANES), f32)
        tot_t = jax.ShapeDtypeStruct((rows, T), f32)
        whole = X // SUB if kept else 8
        n_held = rows if kept else 1 + rows
        spare = [] if kept else [pltpu.VMEM((X, T), f32)]

        def blocks(held_refs, made):
            def get(i):
                if kept:
                    return held_refs[i]
                made[0][...] = kernel_block(held_refs[0][...], held_refs[1 + i][...])
                return made[0]

            return get

        own = call(
            ext_kernel,
            jax.ShapeDtypeStruct((EXT, ny + nx), bf16),
            [
                pltpu.with_memory_space_constraint(t, pltpu.HBM)
                for t in (x_src, y_tgt, a_src, b_tgt)
            ],
            [
                pltpu.VMEM((D, nx), bf16),
                pltpu.VMEM((D, ny), bf16),
                pltpu.VMEM((nx,), bf16),
                pltpu.VMEM((ny,), bf16),
                pltpu.VMEM((EXT, nx), f32),
                pltpu.VMEM((EXT, ny), f32),
                pltpu.SemaphoreType.DMA((4,)),
            ],
            spec=ANY,
        )
        line = [own] + [
            lax.ppermute(own, ("row", "col"), xor_perm(rows * cols, cols + m))
            for m in range(1, cols)
        ]
        both = jnp.concatenate(
            [p[:, 0:ny] for p in line] + [p[:, ny:] for p in line], axis=1
        )
        y0 = both[:, 0:T]
        y, ks = [None] * rows, [None] * rows
        y[0], xe = both[:, 0:T], both[:, T:]

        def start_kernel(e, y_ref, xt, ab, acc, *k):
            xt[...] = jnp.transpose(e[...].astype(f32)).astype(bf16)
            ab[...] = jnp.broadcast_to(xt[:, A_ROW : A_ROW + 1].astype(f32), ab.shape)
            acc[...] = make_blocks(xt, [y_ref], k, jnp.zeros(acc.shape, f32))

        def more_kernel(n, xt, acc, *refs):
            refs[n][...] = make_blocks(xt, refs[:n], refs[n + 1 :], acc[...])

        def more(new, acc):
            cost = pl.CostEstimate(flops=1, bytes_accessed=1, transcendentals=0)
            acc, *k = call(
                lambda *refs: more_kernel(len(new), *refs),
                [lanes_t] + [held((X, T), f32)] * (len(new) * kept),
                [xt, acc] + [y[i] for i in new],
                cost=cost,
            )
            if kept:
                for i, t in zip(new, k):
                    ks[i] = t
            return acc

        raw = {m: swap(y[0], m) for m in (*range(2, rows - 2, 2), rows - 1)}
        y[1] = swap(y[0], 1)
        xt, ab, acc, *k = call(
            start_kernel,
            [held((X, EXT), bf16), lanes_t, lanes_t] + [held((X, T), f32)] * kept,
            [xe, y[0]],
            cost=pl.CostEstimate(flops=1, bytes_accessed=1, transcendentals=0),
        )
        if kept:
            ks[0] = k[0]
        acc = more([1], acc)
        early, late = list(raw)[:-1], list(raw)[-1:]
        for some, others in ((early, []), (late, [m ^ 1 for m in early])):
            *lines, acc = lax.optimization_barrier((*[raw[m] for m in some], acc))
            for m, t in zip(some, lines):
                y[m] = t
                y[m ^ 1] = swap(t, 1)
            acc = more(some + others, acc)
        acc = more([m ^ 1 for m in late], acc)
        matrix = ks if kept else [xt, *y]

        def column_sums(k, u, tot, unroll, z=None):
            for i in range(rows):
                s = col_pass(k(i), u, T, unroll, z if z is None else z.at[i])
                tot[i : i + 1, :] = jnp.sum(s, axis=0, keepdims=True)

        def first_sums(*refs):
            r = Refs(refs)
            acc, ab, kr, tot, u = r.take(ONE, ONE, n_held, ONE, ONE)
            scaling(ab, acc, u)
            column_sums(blocks(kr, r.refs), u, tot, whole)

        tot = call(first_sums, tot_t, [acc, ab, *matrix], [lanes_s] + spare)

        def add_swapped(t, gs, masks):
            def row(i):
                return sum((g[i ^ m : (i ^ m) + 1] for g, m in zip(gs, masks)), t[i : i + 1])

            return jnp.concatenate([row(i) for i in range(rows)], axis=0)

        def add_kernel(t, g, o, send):
            o[...] = add_swapped(t[...], [g[...]], [1])
            send[...] = o[...].astype(bf16)

        tot, send = call(
            add_kernel,
            [tot_t, jax.ShapeDtypeStruct((rows, T), bf16)],
            [tot, swap(tot, 1)],
        )
        got = [swap(send, m) for m in far]

        n_tot = rows * per_row

        def pack_tot(t):
            return jnp.concatenate(
                [t[:, g * width : (g + 1) * width] for g in range(per_row)], axis=0
            ).astype(bf16)

        def unpack_tot(s):
            s = s.astype(f32)
            return jnp.concatenate(
                [s[g * rows : (g + 1) * rows, :] for g in range(per_row)], axis=1
            )

        def second_rows(*refs):
            r = Refs(refs)
            t, gs, ab, bs, kr = r.take(ONE, len(far), ONE, rows, n_held)
            u, acc = r.take(ONE, ONE)
            k = blocks(kr, r.refs)
            total = add_swapped(t[...], [g[...].astype(f32) for g in gs], far)
            acc[...] = jnp.zeros_like(acc)
            for i in range(rows):
                v = bs[i][B_ROW : B_ROW + 1, :].astype(f32) / total[i : i + 1, :]
                row_pass(k(i), jnp.broadcast_to(v, (SUB, T)), acc, 64)
            scaling(ab, acc, u)

        u = call(
            second_rows,
            lanes_t,
            [tot, *got, ab, *y, *matrix],
            [lanes_s] + spare,
        )

        def second_cols(*refs):
            r = Refs(refs)
            u, x, kr = r.take(ONE, ONE, n_held)
            tot_o, keep_o, send_o, z = r.take(ONE, ONE, ONE, ONE)
            column_sums(blocks(kr, r.refs), u, tot_o, 64, z)

            def weighted(mask):
                return jnp.dot(x[...], z[mask], preferred_element_type=f32)

            send_o[0:n_tot, :] = pack_tot(tot_o[...])
            for n, mask in enumerate(ends):
                keep_o[n, :, 0:ny] = weighted(mask)
                at = n_tot + n * EXT
                send_o[at : at + EXT, 0:ny] = weighted(mask ^ 1).astype(bf16)

        tot, keep, send = call(
            second_cols,
            (
                tot_t,
                jax.ShapeDtypeStruct((len(ends), EXT, width), f32),
                jax.ShapeDtypeStruct((n_tot + len(ends) * EXT, width), bf16),
            ),
            [u, xe, *matrix],
            [pltpu.VMEM((rows, X, ny), bf16)] + spare,
        )

        def join(t, kp, g, tot_o, keep_o, *sends):
            tot_o[...] = add_swapped(t[...], [unpack_tot(g[0:n_tot, :])], [1])
            packed = pack_tot(tot_o[...])
            for n in range(len(ends)):
                s = kp[n] + g[n_tot + n * EXT : n_tot + (n + 1) * EXT, :].astype(f32)
                if n == 0:
                    keep_o[...] = s
                else:
                    sends[n - 1][0:n_tot, :] = packed
                    sends[n - 1][n_tot:, :] = s.astype(bf16)

        tot, keep, *send = call(
            join,
            [tot_t, jax.ShapeDtypeStruct((EXT, width), f32)]
            + [jax.ShapeDtypeStruct((n_tot + EXT, width), bf16)] * len(far),
            [tot, keep, swap(send, 1)],
        )
        got = [swap(t, m) for t, m in zip(send, far)]

        def final(*refs):
            r = Refs(refs)
            t, kp, gs, xt, ys = r.take(ONE, ONE, len(far), ONE, rows)
            kr, src_o, tgt_o = r.take(rows * kept, ONE, ONE)
            total = add_swapped(t[...], [unpack_tot(g[0:n_tot, :]) for g in gs], far)
            num = sum((g[n_tot:, :].astype(f32) for g in gs), kp[...])
            tgt_o[...] = num[0:D, 0:ny] / total[0:1, 0:ny]
            res = jnp.zeros((nx, EXT), f32)
            for i in range(rows):
                yi = ys[i][...]
                v = yi[B_ROW : B_ROW + 1, :].astype(f32) / total[i : i + 1, :]
                e = kr[i][0:nx, :] if kept else kernel_block(xt[0:nx, :], yi)
                res = res + lax.dot_general(
                    (e * v).astype(bf16),
                    yi,
                    (((1,), (1,)), ((), ())),
                    preferred_element_type=f32,
                )
            res = jnp.transpose(res)
            src_o[...] = res[0:D, :] / res[NORM_X : NORM_X + 1, :]

        return tuple(
            call(
                final,
                (
                    jax.ShapeDtypeStruct((D, nx), f32),
                    jax.ShapeDtypeStruct((D, ny), f32),
                ),
                [tot, keep, *got, xt, *y, *(ks if kept else [])],
            )
        )

    spec = P(None, ("row", "col"))
    vec = P(("row", "col"))
    return jax.shard_map(
        per_device,
        mesh=mesh,
        in_specs=(spec, spec, vec, vec),
        out_specs=(spec, spec),
        check_vma=False,
    )
```
